32 devices in a mesh: scen: 8 (over y, x, core), grp: 4 (over z).
Axes of the slice: x: 2, y: 2, z: 4, core: 2. Of those that a mesh axis runs over, the one named last changes fastest.
Arguments:
- coupling: bfloat16 [32, 768, 4096], P(('scen', 'grp')), may hold values from -1.5 to 1.5
- scen_kkt: bfloat16 [32, 768, 768], P(('scen', 'grp')), may hold values from -3 to 5, as said below
- active_rows: int32 [32], P(('scen', 'grp')), may hold values from 128 to 768, as said below
- first_hess: float32 [512], replicated, may hold values from 20 to 400
Outputs:
- factor_panels: float32 [4096, 512], P('scen')
The draws below stay inside these ranges and needn't reach their ends.
Inputs may be any that keep to these rules, and one draw needn't show every extreme that they name: `scen_kkt`: each block is symmetric positive definite: a Gram matrix of 768 columns divided by 768 plus a positive diagonal. `active_rows`: each count is a multiple of 128; some scenario has 768 and some has 128.
All inputs are finite; a program needn't handle non-finite values.
Results may differ from the reference program's by a relative error of at most 0.0011.
Values sent between devices are 32-bit elements; how exact they have to be, the bound alone decides.
No kernel may reach another device: no remote copies, remote signals or barrier semaphores. Data moves between devices by JAX's collectives and lax.ppermute only.
A program may use at most 64 MiB of HBM per device.

```python
import math
import jax
import jax.numpy as jnp
from jax import lax

NB = 768
NC = 4096
PW = 256
TILE = 128
NSCEN = 32


def draw_scen_kkt(key, part):
    key_gram = jax.random.fold_in(key, 11)
    key_diag = jax.random.fold_in(key, 12)
    bound_value = math.sqrt(3.0)
    gram_src = jax.random.uniform(key_gram, (NSCEN, NB, NB), jnp.float32, -bound_value, bound_value)
    gram = jnp.einsum('sij,skj->sik', gram_src, gram_src) / NB
    offset_diag = jnp.exp(jax.random.uniform(key_diag, (NSCEN, NB), jnp.float32, math.log(0.02), math.log(0.5)))
    identity = jnp.eye(NB, dtype=jnp.float32)
    return (gram + offset_diag[:, :, None] * identity).astype(jnp.bfloat16)


def draw_active_rows(key, part):
    key_tiles = jax.random.fold_in(key, 21)
    key_order = jax.random.fold_in(key, 22)
    tiles = jax.random.randint(key_tiles, (NSCEN,), 1, NB // TILE + 1)
    order = jax.random.permutation(key_order, NSCEN)
    tiles = tiles.at[order[0]].set(NB // TILE)
    tiles = tiles.at[order[1]].set(1)
    return (tiles * TILE).astype(jnp.int32)


def raised(array, own_key, source, target, blocks, factor):
    owner, partner = [(jnp.arange(array.shape[position]) // (array.shape[position] // blocks)).reshape([-1 if axis == position else 1 for axis in range(array.ndim)]) for position in (source, target)]
    chosen = jax.random.permutation(own_key, blocks)[partner]
    strong = (owner == chosen) | (owner == (partner + blocks // 2) % blocks)
    return jnp.where(strong, factor * array, array)


def steps_of(stream_key, extent, pieces, least, high):
    gain = 1.0
    for dim, blocks in pieces:
        steps = jax.random.uniform(jax.random.fold_in(jax.random.fold_in(stream_key, 6), dim), (blocks,), jnp.float32, least / len(pieces), high / len(pieces))
        gain = gain * jnp.repeat(jnp.exp(steps), extent[dim] // blocks).reshape((-1,) + (1,) * (len(extent) - 1 - dim))
    return gain


def noise_with(key, shape, scale, reach, pieces, heavy, kind=jnp.bfloat16):
    drawn = scale * jax.random.normal(key, shape, jnp.float32)
    if pieces:
        drawn = drawn * steps_of(key, shape, pieces, -0.22, 0.18)
    return jnp.clip(raised(drawn, jax.random.fold_in(key, 3), *heavy), -reach, reach).astype(kind)


def setup_inputs(seed: int = 0) -> dict:
    key_of = jax.random.split(jax.random.key(seed), 5)
    return {
        "coupling": noise_with(key_of[0], (NSCEN, NB, NC), 0.25, 1.5, ((0, 32),), (0, 2, 32, 2.75)),
        "scen_kkt": draw_scen_kkt(jax.random.fold_in(key_of[4], 71), 0),
        "active_rows": draw_active_rows(jax.random.fold_in(key_of[4], 71), 0),
        "first_hess": jnp.clip(jnp.exp(jax.random.uniform(key_of[3], (2 * PW,), jnp.float32, math.log(20.0), math.log(400.0))), 20.0, 400.0),
    }


def solve_block(factor, right_side):
    return jax.scipy.linalg.cho_solve((factor, True), right_side)

def solve_right(lower_tri, rows):
    return jax.scipy.linalg.solve_triangular(lower_tri, rows.T, lower=True).T

def reference(coupling, scen_kkt, active_rows, first_hess):
    panel_cols = 2 * PW

    def add_scenario(running, scen_items):
        scen_block, kkt_block, active = scen_items
        keep_mask = (jnp.arange(NB, dtype=jnp.int32)[:, None] < active).astype(jnp.float32)
        coupling_panel = scen_block[:, :panel_cols].astype(jnp.float32) * keep_mask
        factor = jnp.linalg.cholesky(kkt_block.astype(jnp.float32))
        solved = (solve_block(factor, coupling_panel) * keep_mask).astype(jnp.bfloat16)
        term = jnp.dot(scen_block.astype(jnp.float32).T, solved.astype(jnp.float32), precision=lax.Precision.HIGHEST)
        return (running + term, None)
    start_panel = jnp.zeros((NC, panel_cols), jnp.float32)
    schur_panel, ignored = lax.scan(add_scenario, start_panel, (coupling, scen_kkt, active_rows))
    row_ids = jnp.arange(NC, dtype=jnp.int32)[:, None]
    col_ids = jnp.arange(panel_cols, dtype=jnp.int32)[None, :]
    schur_panel = schur_panel + jnp.where(row_ids == col_ids, first_hess[None, :], jnp.zeros((), jnp.float32))
    diag_one = jnp.linalg.cholesky(schur_panel[:PW, :PW])
    lower_one = solve_right(diag_one, schur_panel[PW:, :PW])
    updated = schur_panel[PW:, PW:] - jnp.dot(lower_one, lower_one[:PW].T, precision=lax.Precision.HIGHEST)
    diag_two = jnp.linalg.cholesky(updated[:PW])
    lower_two = solve_right(diag_two, updated[PW:])
    left_half = jnp.concatenate([diag_one, lower_one], 0)
    right_half = jnp.concatenate([jnp.zeros((PW, PW), jnp.float32), diag_two, lower_two], 0)
    return jnp.concatenate([left_half, right_half], 1)
```

```python
import jax
import jax.numpy as jnp
from jax import lax
from jax.experimental import pallas as pl
from jax.experimental.pallas import tpu as pltpu
from jax.sharding import PartitionSpec as P

H=lax.Precision.HIGHEST
def bc(x,s): return jnp.broadcast_to(x[s:s+1,:], x.shape)
def elim(R, off, nb):
    ng=nb//8; nh=len(R[0])
    row=lax.broadcasted_iota(jnp.int32,(8,128),0)
    L={}
    for j in range(nb):
        for g in range(j//8,ng):
            L[j,g]=jnp.broadcast_to(R[g][0][:,off+j:off+j+1],(8,128))
    out=[]
    for g in range(ng): out.append(None)
    for j in range(0,nb,2):
        gj=j//8; s=j%8
        a=bc(L[j,gj],s); b=bc(L[j,gj],s+1); c=bc(L[j+1,gj],s+1)
        det=a*c-b*b
        rd=1.0/det
        al={}; be={}
        for g in range(gj,ng):
            x=L[j,g]*c-L[j+1,g]*b; y=L[j+1,g]*a-L[j,g]*b
            if g==gj:
                x=jnp.where(row>s+1,x,0.0); y=jnp.where(row>s+1,y,0.0)
            al[g]=x; be[g]=y
        for k in range(j+2,nb):
            p=bc(L[j,k//8],k%8); q=bc(L[j+1,k//8],k%8)
            for g in range(k//8,ng):
                L[k,g]=L[k,g]-(al[g]*p+be[g]*q)*rd
        r1=[bc(R[gj][h],s) for h in range(nh)]; r2=[bc(R[gj][h],s+1) for h in range(nh)]
        ra=1.0/a
        sa=lax.rsqrt(a); sb=lax.rsqrt(det*ra); ba=b*ra
        if s==0: out[gj]=[jnp.zeros((8,128),jnp.float32)]*nh
        for h in range(nh):
            out[gj][h]=jnp.where(row==s,r1[h]*sa,jnp.where(row==s+1,(r2[h]-ba*r1[h])*sb,out[gj][h]))
        for g in range(gj,ng):
            if g==gj and s==6: continue
            x=al[g]*rd; y=be[g]*rd
            R[g]=[R[g][h]-(x*r1[h]+y*r2[h]) for h in range(nh)]
    return out
def base128(A, nb=32, prec=H):
    row=lax.broadcasted_iota(jnp.int32,(8,128),0); lane=lax.broadcasted_iota(jnp.int32,(8,128),1)
    M=[[A[8*g:8*g+8,:],jnp.where(lane==row+8*g,1.0,0.0)] for g in range(16)]
    outs=[]
    n=128//nb; ng=nb//8
    for c in range(n):
        o=elim(M[c*ng:(c+1)*ng],c*nb,nb)
        outs+=o
        if c<n-1:
            O=[jnp.concatenate([o[g][h] for g in range(ng)],0) for h in range(2)]
            for h in range(2):
                T=lax.dot_general(O[0],O[h],(((0,),(0,)),((),())),precision=prec,preferred_element_type=jnp.float32)
                for g in range((c+1)*ng,16):
                    M[g][h]=M[g][h]-T[8*g:8*g+8]
    return [jnp.concatenate([outs[g][h] for g in range(16)],0) for h in range(2)]
def dotT(a,b,prec=H): return lax.dot_general(a,b,(((0,),(0,)),((),())),precision=prec,preferred_element_type=jnp.float32)
def dot(a,b,prec=H): return lax.dot_general(a,b,(((1,),(0,)),((),())),precision=prec,preferred_element_type=jnp.float32)
BS=128
def scen_kernel(act_ref,k_ref,c_ref,x_ref,A,Z,W):
    n=k_ref.shape[1]; nblk=n//BS
    act=act_ref[0]
    def keep(k):
        r=lax.broadcasted_iota(jnp.int32,(BS,1),0)+k*BS
        return r<act
    blk=lambda k: slice(k*BS,(k+1)*BS)
    for k in range(nblk):
        Akk=k_ref[0,blk(k),blk(k)].astype(jnp.float32) if k==0 else A[blk(k),blk(k)]
        _,Wk=base128(Akk)
        W[k]=Wk
        if k<nblk-1:
            src=k_ref[0,blk(k),(k+1)*BS:].astype(jnp.float32) if k==0 else A[blk(k),(k+1)*BS:]
            P=dot(Wk,src)
            A[blk(k),(k+1)*BS:]=P
            for i in range(k+1,nblk):
                o=(i-k-1)*BS
                old=k_ref[0,blk(i),i*BS:].astype(jnp.float32) if k==0 else A[blk(i),i*BS:]
                A[blk(i),i*BS:]=old-dotT(P[:,o:o+BS],P[:,o:])
        rhs=jnp.where(keep(k),c_ref[0,blk(k),:].astype(jnp.float32),0.0)
        if k>0: rhs=rhs-dotT(A[0:k*BS,blk(k)],Z[0:k*BS,:])
        Z[blk(k),:]=dot(Wk,rhs)
    for k in reversed(range(nblk)):
        z=Z[blk(k),:]
        if k<nblk-1: z=z-dot(A[blk(k),(k+1)*BS:],Z[(k+1)*BS:,:])
        x=dotT(W[k],z)
        Z[blk(k),:]=x
        x_ref[blk(k),:]=jnp.where(keep(k),x,0.0).astype(jnp.bfloat16)
def scen_solve(kkt,coupling,active,cols):
    n=kkt.shape[1]
    return pl.pallas_call(scen_kernel,
        out_shape=jax.ShapeDtypeStruct((n,cols),jnp.bfloat16),
        in_specs=[pl.BlockSpec(memory_space=pltpu.SMEM),pl.BlockSpec((1,n,n),lambda i:(0,0,0)),pl.BlockSpec((1,n,cols),lambda i:(0,0,0))],
        out_specs=pl.BlockSpec((n,cols),lambda i:(0,0)),
        grid=(1,),
        scratch_shapes=[pltpu.VMEM((n,n),jnp.float32),pltpu.VMEM((n,cols),jnp.float32),pltpu.VMEM((n//BS,BS,BS),jnp.float32)],
        compiler_params=pltpu.CompilerParams(vmem_limit_bytes=48*2**20),
        name="scen_solve")(active,kkt,coupling)
def pivot_kernel(s_ref,w_ref,A):
    n=s_ref.shape[0]; nblk=n//BS
    blk=lambda k: slice(k*BS,(k+1)*BS)
    for k in range(nblk):
        _,Wk=base128(s_ref[blk(k),blk(k)] if k==0 else A[blk(k),blk(k)])
        if k<nblk-1:
            P=dot(Wk,s_ref[blk(k),(k+1)*BS:] if k==0 else A[blk(k),(k+1)*BS:])
            A[blk(k),(k+1)*BS:]=P
            for i in range(k+1,nblk):
                o=(i-k-1)*BS
                old=s_ref[blk(i),i*BS:] if k==0 else A[blk(i),i*BS:]
                A[blk(i),i*BS:]=old-dotT(P[:,o:o+BS],P[:,o:])
            w_ref[blk(k),(k+1)*BS:]=jnp.zeros((BS,n-(k+1)*BS),jnp.float32)
        w_ref[blk(k),blk(k)]=Wk
        if k>0:
            w_ref[blk(k),0:k*BS]=-dot(Wk,dotT(A[0:k*BS,blk(k)],w_ref[0:k*BS,0:k*BS]))
def pivot_inv(s):
    n=s.shape[0]
    return pl.pallas_call(pivot_kernel,out_shape=jax.ShapeDtypeStruct((n,n),jnp.float32),
        scratch_shapes=[pltpu.VMEM((n,n),jnp.float32)],
        compiler_params=pltpu.CompilerParams(vmem_limit_bytes=32*2**20),name="pivot_inv")(s)


PW = 256


def per_device(coupling, scen_kkt, active_rows, first_hess):
    _, _, coupled = coupling.shape
    own_rows = coupled // lax.axis_size("scen")
    scen_idx = lax.axis_index("scen")
    panel_cols = 2 * PW
    solved = scen_solve(scen_kkt, coupling, active_rows, panel_cols)
    pivot = dotT(coupling[0, :, :panel_cols], solved, None)
    pivot = lax.psum(pivot, ("scen", "grp")) + jnp.diag(first_hess)
    own_panel = lax.psum_scatter(
        dotT(coupling[0], solved, None), "scen", scatter_dimension=0, tiled=True
    )
    own_panel = lax.psum(own_panel, "grp")
    global_row = scen_idx * own_rows + lax.broadcasted_iota(jnp.int32, (own_rows, 1), 0)
    col_ids = lax.broadcasted_iota(jnp.int32, (1, panel_cols), 1)
    own_panel = own_panel + jnp.where(global_row == col_ids, first_hess[None, :], 0.0)
    inv = pivot_inv(pivot)
    rows = lax.dot_general(
        own_panel, inv, (((1,), (1,)), ((), ())), precision=H, preferred_element_type=jnp.float32
    )
    return jnp.where(global_row < col_ids, 0.0, rows)


def solution(mesh):
    placed = (
        P(("scen", "grp"), None, None),
        P(("scen", "grp"), None, None),
        P(("scen", "grp")),
        P(),
    )
    return jax.shard_map(
        per_device, mesh=mesh, in_specs=placed, out_specs=P("scen", None), check_vma=False
    )
```

```python
import jax
import jax.numpy as jnp
from jax import lax
from jax.experimental import pallas as pl
from jax.experimental.pallas import tpu as pltpu
from jax.sharding import PartitionSpec as P

H=lax.Precision.HIGHEST
def bc(x,s): return jnp.broadcast_to(x[s:s+1,:], x.shape)
def halves(x):
    hi=x.astype(jnp.bfloat16)
    return hi,(x-hi.astype(jnp.float32)).astype(jnp.bfloat16)
def dot3(a,b,dims):
    (i,),(j,)=dims
    ah,al=halves(a); bh,bl=halves(b)
    return lax.dot_general(jnp.concatenate([ah,ah,al],i),jnp.concatenate([bh,bl,bh],j),(dims,((),())),preferred_element_type=jnp.float32)
def elim(R, off, nb):
    ng=nb//8; nh=len(R[0])
    row=lax.broadcasted_iota(jnp.int32,(8,128),0)
    L={}
    for j in range(nb):
        for g in range(j//8,ng):
            L[j,g]=jnp.broadcast_to(R[g][0][:,off+j:off+j+1],(8,128))
    out=[None]*ng
    a=bc(L[0,0],0); b=bc(L[0,0],1); c=bc(L[1,0],1)
    for j in range(0,nb,2):
        gj=j//8; s=j%8
        det=a*c-b*b
        rd=1.0/det
        al={}; be={}
        for g in range(gj,ng):
            x=L[j,g]*c-L[j+1,g]*b; y=L[j+1,g]*a-L[j,g]*b
            if g==gj:
                x=jnp.where(row>s+1,x,0.0); y=jnp.where(row>s+1,y,0.0)
            al[g]=x; be[g]=y
        nxt=None
        if j+2<nb:
            k=j+2; g=k//8; t=k%8
            p,q,p2,q2=bc(L[j,g],t),bc(L[j+1,g],t),bc(L[j,g],t+1),bc(L[j+1,g],t+1)
            x,y,x2,y2=bc(al[g],t),bc(be[g],t),bc(al[g],t+1),bc(be[g],t+1)
            nxt=(bc(L[k,g],t)-(x*p+y*q)*rd, bc(L[k,g],t+1)-(x2*p+y2*q)*rd, bc(L[k+1,g],t+1)-(x2*p2+y2*q2)*rd)
        for k in range(j+2,nb):
            p=bc(L[j,k//8],k%8); q=bc(L[j+1,k//8],k%8)
            for g in range(k//8,ng):
                L[k,g]=L[k,g]-(al[g]*p+be[g]*q)*rd
        r1=[bc(R[gj][h],s) for h in range(nh)]; r2=[bc(R[gj][h],s+1) for h in range(nh)]
        ra=1.0/a
        sa=lax.rsqrt(a); sb=lax.rsqrt(det*ra); ba=b*ra
        if s==0: out[gj]=[jnp.zeros((8,128),jnp.float32)]*nh
        for h in range(nh):
            out[gj][h]=jnp.where(row==s,r1[h]*sa,jnp.where(row==s+1,(r2[h]-ba*r1[h])*sb,out[gj][h]))
        for g in range(gj,ng):
            if g==gj and s==6: continue
            x=al[g]*rd; y=be[g]*rd
            R[g]=[R[g][h]-(x*r1[h]+y*r2[h]) for h in range(nh)]
        if nxt: a,b,c=nxt
    return out
def base128(A, exact=False, nb=32, between=None):
    row=lax.broadcasted_iota(jnp.int32,(8,128),0); lane=lax.broadcasted_iota(jnp.int32,(8,128),1)
    M=[[A[8*g:8*g+8,:],jnp.where(lane==row+8*g,1.0,0.0)] for g in range(16)]
    outs=[]
    n=128//nb; ng=nb//8
    for c in range(n):
        if between: between[c]()
        o=elim(M[c*ng:(c+1)*ng],c*nb,nb)
        outs+=o
        if c<n-1:
            O=[jnp.concatenate([o[g][h] for g in range(ng)],0) for h in range(2)]
            O2=jnp.concatenate(O,1)
            dims=((0,),(0,))
            if exact: T=lax.dot_general(O[0],O2,(dims,((),())),precision=H,preferred_element_type=jnp.float32)
            else: T=dot3(O[0],O2,dims)
            for g in range((c+1)*ng,16):
                M[g]=[M[g][h]-T[8*g:8*g+8,128*h:128*h+128] for h in range(2)]
    return [jnp.concatenate([outs[g][h] for g in range(16)],0) for h in range(2)]
BS=128
def dotT(a,b,prec=H): return lax.dot_general(a,b,(((0,),(0,)),((),())),precision=prec,preferred_element_type=jnp.float32)
def dot(a,b,prec=H): return lax.dot_general(a,b,(((1,),(0,)),((),())),precision=prec,preferred_element_type=jnp.float32)
def scen_kernel(act_ref,k_ref,c_hbm,x_ref,M,D,Wk,left,right,row_ref,inv_ref,panel_ref,sem):
    n=k_ref.shape[1]; nblk=n//BS
    fetch=pltpu.make_async_copy(c_hbm.at[0,:,0:panel_ref.shape[1]],panel_ref,sem)
    fetch.start()
    M[...]=k_ref[0].astype(jnp.float32)
    D[...]=k_ref[0,0:BS,0:BS].astype(jnp.float32)
    Wk[...]=jnp.zeros_like(Wk)
    eye=jnp.where(lax.broadcasted_iota(jnp.int32,(BS,BS),0)==lax.broadcasted_iota(jnp.int32,(BS,BS),1),1.0,0.0)
    def sweep(k,live):
        here=pl.ds(pl.multiple_of(k*BS,BS),BS)
        def invert():
            W=Wk[...]
            inv_ref[...]=dotT(W,W)
            col_hi,col_lo=halves(jnp.where(live,M[:,here],0.0))
            left[:,0:BS]=col_hi; left[:,BS:2*BS]=col_hi; left[:,2*BS:]=col_lo
            left[here,:]=jnp.zeros((BS,3*BS),jnp.bfloat16)
        def scale():
            inv=inv_ref[...]
            row=dot3(inv,M[here,:],((1,),(0,)))
            row_ref[...]=row
            row_ref[:,here]=eye-inv
            hi,lo=halves(row_ref[...])
            right[0:BS,:]=hi; right[BS:2*BS,:]=lo; right[2*BS:,:]=hi
            row_ref[...]=row
            row_ref[:,here]=-inv
        def spread(rows):
            M[rows,:]=M[rows,:]-dot(left[rows,:],right[...],None)
        def first(): spread(slice(0,n//2))
        def second():
            spread(slice(n//2,n))
            M[here,:]=jnp.where(live,row_ref[...],M[here,:])
        return invert,scale,first,second
    def step(k,_):
        here=pl.ds(pl.multiple_of(k*BS,BS),BS)
        follow=pl.ds(pl.multiple_of(jnp.minimum(k+1,nblk-1)*BS,BS),BS)
        _,W=base128(D[...],between=sweep(jnp.maximum(k-1,0),k>0))
        P=dot3(W,M[here,follow],((1,),(0,)))
        D[...]=M[follow,follow]-dot3(P,P,((0,),(0,)))
        Wk[...]=W
        return 0
    lax.fori_loop(0,nblk,step,0)
    for part in sweep(nblk-1,True): part()
    fetch.wait()
    kept=lax.broadcasted_iota(jnp.int32,(n,1),0)<act_ref[0]
    panel=jnp.where(kept,panel_ref[...],jnp.zeros((),jnp.bfloat16))
    hi,lo=halves(M[...])
    x=dotT(panel,hi,None)+dotT(panel,lo,None)
    kept=lax.broadcasted_iota(jnp.int32,(1,n),1)<act_ref[0]
    x_ref[...]=jnp.where(kept,-x,0.0).astype(jnp.bfloat16)
def scen_solve(kkt,coupling,active,cols):
    n=kkt.shape[1]
    vm=pltpu.VMEM
    return pl.pallas_call(scen_kernel,
        out_shape=jax.ShapeDtypeStruct((cols,n),jnp.bfloat16),
        in_specs=[pl.BlockSpec(memory_space=pltpu.SMEM),pl.BlockSpec(memory_space=vm),pl.BlockSpec(memory_space=pl.ANY)],
        out_specs=pl.BlockSpec(memory_space=vm),
        scratch_shapes=[vm((n,n),jnp.float32),vm((BS,BS),jnp.float32),vm((BS,BS),jnp.float32),vm((n,3*BS),jnp.bfloat16),
            vm((3*BS,n),jnp.bfloat16),vm((BS,n),jnp.float32),vm((BS,BS),jnp.float32),vm((n,cols),jnp.bfloat16),pltpu.SemaphoreType.DMA],
        compiler_params=pltpu.CompilerParams(vmem_limit_bytes=48*2**20),
        name="scen_solve")(active,kkt,coupling)
def blk(k): return slice(k*BS,(k+1)*BS)
def sym(a): return 0.5*(a+a.T)
def upper_blocks(m): return [(i,j) for i in range(m) for j in range(i,m)]
def packed_places(m):
    places,slots={},[]
    blocks=upper_blocks(m)
    full=len(blocks)//m*m
    for q,ij in enumerate(blocks[:full]): places[ij]=[(0,q//m*BS,q%m,BS)]
    rest=blocks[full:]
    cut=BS*len(rest)//m
    for q,ij in enumerate(rest):
        per=BS//cut
        places[ij]=[(t*cut,full//m*BS,q*per+t,cut) for t in range(per)]
    return places,full//m*BS+(cut if rest else 0)
def lanes(g): return slice(g*BS,(g+1)*BS)
def pivot_prod_kernel(xt_ref,c_ref,o_ref):
    n=xt_ref.shape[0]; half=n//2; per=half//BS
    T=dot(xt_ref[...],c_ref[0],None)
    D=[sym(T[:half,:half]),sym(T[half:,half:])]
    for (i,j),where in packed_places(n//BS)[0].items():
        if i//per==j//per: v=D[i//per][blk(i%per),blk(j%per)]
        else: v=T[blk(i),blk(j)]
        for r,row,g,rows in where: o_ref[row:row+rows,lanes(g)]=v[r:r+rows,:]
def pivot_prod(xt,coupling):
    cols,n=xt.shape
    high=packed_places(cols//BS)[1]
    return pl.pallas_call(pivot_prod_kernel,
        out_shape=jax.ShapeDtypeStruct((high,cols),jnp.float32),grid=(1,),
        in_specs=[pl.BlockSpec((cols,n),lambda i:(0,0)),pl.BlockSpec((1,n,cols),lambda i:(0,0,0))],
        out_specs=pl.BlockSpec((high,cols),lambda i:(0,0)),
        compiler_params=pltpu.CompilerParams(vmem_limit_bytes=48*2**20),
        cost_estimate=pl.CostEstimate(flops=2*cols*cols*n,bytes_accessed=4*cols*n+4*high*cols,transcendentals=0),
        name="pivot_prod")(xt,coupling)
def panel_factor(A,wt_ref,l_ref,base):
    n=A.shape[1]; end=base+2*BS
    eye=lax.broadcasted_iota(jnp.int32,(BS,BS),0)<=lax.broadcasted_iota(jnp.int32,(BS,BS),1)
    WT=[]
    for k in range(2):
        lo=base+k*BS; me=slice(lo,lo+BS)
        Uk,Wk=base128(A[me,me])
        WT.append(Wk.T)
        l_ref[lo-base:lo-base+BS,blk(k)]=jnp.where(eye,Uk,0.0).T
        if lo+BS<n:
            P=dot3(Wk,A[me,lo+BS:],((1,),(0,)))
            A[me,lo+BS:]=P
            for i in range((n-lo)//BS-1):
                r=lo+(i+1)*BS
                if r<end: A[r:r+BS,r:]=A[r:r+BS,r:]-dot3(P[:,i*BS:(i+1)*BS],P[:,i*BS:],((0,),(0,)))
                l_ref[r-base:r-base+BS,blk(k)]=P[:,i*BS:(i+1)*BS].T
    l_ref[0:BS,blk(1)]=jnp.zeros((BS,BS),jnp.float32)
    top=wt_ref.shape[0]-2*BS
    wt_ref[top:top+BS,blk(0)]=WT[0]
    wt_ref[top+BS:,blk(0)]=jnp.zeros((BS,BS),jnp.float32)
    wt_ref[top:top+BS,blk(1)]=-dot(dot(WT[0],A[base:base+BS,base+BS:end]),WT[1])
    wt_ref[top+BS:,blk(1)]=WT[1]
def pivot_one_kernel(perm_ref,hess_ref,*refs):
    srcs,(wt_ref,l_ref,u_ref,rest_ref,A,pk)=refs[:-6],refs[-6:]
    n=A.shape[0]; nblk=n//BS; half=n//2
    each=perm_ref.shape[0]//len(srcs)
    rows=srcs[0].shape[0]//each
    for s,src in enumerate(srcs):
        for q in range(each):
            dst=pl.multiple_of(perm_ref[s*each+q]*rows,8)
            pk[pl.ds(dst,rows),:]=src[q*rows:(q+1)*rows,:]
    diag=lax.broadcasted_iota(jnp.int32,(BS,BS),0)==lax.broadcasted_iota(jnp.int32,(BS,BS),1)
    for (i,j),where in packed_places(nblk)[0].items():
        parts=[pk[row:row+high,lanes(g)] for _,row,g,high in where]
        v=parts[0] if len(parts)==1 else jnp.concatenate(parts,0)
        A[blk(i),blk(j)]=v+jnp.where(diag,hess_ref[:,blk(i)],0.0) if i==j else v
    panel_factor(A,wt_ref,l_ref,0)
    u=A[0:half,half:]
    u_ref[...]=u
    for k in range(half//BS):
        o=k*BS
        rest_ref[o:o+BS,o:]=A[half+o:half+o+BS,half+o:]-dot3(u[:,o:o+BS],u[:,o:],((0,),(0,)))
    rest_ref[BS:,0:BS]=jnp.zeros((BS,BS),jnp.float32)
def pivot_one(perm,hess,*srcs):
    n=hess.shape[0]; total=sum(s.shape[0] for s in srcs)
    sd=lambda r,c: jax.ShapeDtypeStruct((r,c),jnp.float32)
    vm=pl.BlockSpec(memory_space=pltpu.VMEM)
    return pl.pallas_call(pivot_one_kernel,out_shape=[sd(n//2,n//2),sd(n,n//2),sd(n//2,n//2),sd(n//2,n//2)],
        in_specs=[pl.BlockSpec(memory_space=pltpu.SMEM)]+[vm]*(1+len(srcs)),out_specs=[vm]*4,
        scratch_shapes=[pltpu.VMEM((n,n),jnp.float32),pltpu.VMEM((total,n),jnp.float32)],
        cost_estimate=pl.CostEstimate(flops=10**10,bytes_accessed=4*2**20,transcendentals=0),
        compiler_params=pltpu.CompilerParams(vmem_limit_bytes=16*2**20),name="pivot_one")(perm,hess[None],*srcs)
def pivot_two_kernel(wt1_ref,u_ref,rest_ref,wt_ref,l_ref,A):
    half=wt1_ref.shape[0]
    A[...]=rest_ref[...]
    panel_factor(A,wt_ref,l_ref,0)
    wt_ref[0:half,:]=-dot(wt1_ref[...],dot(u_ref[...],wt_ref[half:,:]))
def pivot_two(wt1,u,rest):
    half=wt1.shape[0]
    sd=lambda r,c: jax.ShapeDtypeStruct((r,c),jnp.float32)
    vm=pl.BlockSpec(memory_space=pltpu.VMEM)
    return pl.pallas_call(pivot_two_kernel,out_shape=[sd(2*half,half),sd(half,half)],
        in_specs=[vm]*3,out_specs=[vm]*2,scratch_shapes=[pltpu.VMEM((half,half),jnp.float32)],
        cost_estimate=pl.CostEstimate(flops=10**10,bytes_accessed=4*2**20,transcendentals=0),
        compiler_params=pltpu.CompilerParams(vmem_limit_bytes=16*2**20),name="pivot_two")(wt1,u,rest)


PW = 256
HALF = 256
CUTS = (0, 72, 168, 256)
UNIT = 40
FIRST = 24
HOPS = {"x": ("scen", 2), "y": ("scen", 4), "z": ("grp", 1)}
ORDERS = ("xyz", "yzx", "zxy")


def flip(array, axis, mask):
    size = lax.axis_size(axis)
    return lax.ppermute(array, axis, [(i, i ^ mask) for i in range(size)])


def after(array, *others):
    return lax.optimization_barrier((array,) + others)[0]


def products_kernel(where_ref, xt_ref, c_ref, packed_ref, a_ref, b_ref, z_ref):
    slab = where_ref[pl.program_id(0)]
    total = dot(xt_ref[...], c_ref[0], None)
    for half in range(2):
        z = where_ref[4] ^ half
        part = total[half * HALF : (half + 1) * HALF, :]
        a_ref[pl.ds(z, 1), : CUTS[1], :] = part[CUTS[0] : CUTS[1], :][None]
        b_ref[0, pl.ds(z, 1), 0] = part[CUTS[1] : CUTS[2], :][None]
        z_ref[pl.ds(z, 1), 0] = part[CUTS[2] : CUTS[3], :][None]
    unit = pl.multiple_of(slab * UNIT, 8)
    a_ref[0, CUTS[1] :, :] = packed_ref[pl.ds(unit, FIRST), :]
    rest = UNIT - FIRST
    a_ref[1, CUTS[1] : CUTS[1] + rest, :] = packed_ref[pl.ds(unit + FIRST, rest), :]
    a_ref[1, CUTS[1] + rest :, :] = jnp.zeros((FIRST - rest, a_ref.shape[2]), jnp.float32)


def panel_products(where, xt, coupling, packed):
    cols, rows = xt.shape
    own = coupling.shape[2] // 8
    high = [CUTS[1] + FIRST, CUTS[2] - CUTS[1], CUTS[3] - CUTS[2]]
    shapes = [(8, high[0], own), (2, 2, 2, high[1], own), (2, 4, high[2], own)]
    pieces = pl.pallas_call(
        products_kernel,
        out_shape=[jax.ShapeDtypeStruct(shape, jnp.float32) for shape in shapes],
        grid_spec=pltpu.PrefetchScalarGridSpec(
            num_scalar_prefetch=1,
            grid=(4,),
            in_specs=[
                pl.BlockSpec((cols, rows), lambda s, w: (0, 0)),
                pl.BlockSpec((1, rows, own), lambda s, w: (0, 0, w[s])),
                pl.BlockSpec(packed.shape, lambda s, w: (0, 0)),
            ],
            out_specs=[
                pl.BlockSpec((2, high[0], own), lambda s, w: (s, 0, 0)),
                pl.BlockSpec((1, 2, 1, high[1], own), lambda s, w: (s % 2, 0, s // 2, 0, 0)),
                pl.BlockSpec((2, 1, high[2], own), lambda s, w: (0, s, 0, 0)),
            ],
        ),
        cost_estimate=pl.CostEstimate(
            flops=8 * own * cols * rows, bytes_accessed=8 * own * (rows + 4 * cols), transcendentals=0
        ),
        compiler_params=pltpu.CompilerParams(vmem_limit_bytes=56 * 2**20),
        name="panel_products",
    )(where, xt, coupling, packed)
    return [p.reshape((8,) + p.shape[-2:]) for p in pieces]


def final_kernel(where_ref, wt1_ref, wt2_ref, l1_ref, l2_ref, mine_ref, other_ref, *refs, part):
    out_ref = refs[-1]

    @pl.when(where_ref[1] == 0)
    def _():
        out_ref[:, :PW] = l1_ref[part * HALF : (part + 1) * HALF, :]
        out_ref[:, PW:] = l2_ref[...] if part else jnp.zeros_like(l2_ref)

    @pl.when(where_ref[1] > 0)
    def _():
        swap = where_ref[0] > 0
        one = jnp.where(swap, other_ref[...], mine_ref[...])
        two = jnp.where(swap, mine_ref[...], other_ref[...])
        out_ref[:, :PW] = dotT(one, wt1_ref[...])
        out_ref[:, PW:] = dotT(one, wt2_ref[:PW, :]) + dotT(two, wt2_ref[PW:, :])


def final_rows(where, inverse, mine, other, part, held=None):
    vmem = pl.BlockSpec(memory_space=pltpu.VMEM)
    block = lambda *shape: pl.BlockSpec(shape, lambda i: (0, 0))
    args = (where, *inverse, mine, other) + (() if held is None else (held,))
    return pl.pallas_call(
        lambda *refs: final_kernel(*refs, part=part),
        out_shape=jax.ShapeDtypeStruct((2 * HALF, 2 * PW), jnp.float32),
        grid=(1,),
        in_specs=[pl.BlockSpec(memory_space=pltpu.SMEM)]
        + [block(*a.shape) for a in args[1:7]]
        + [pl.BlockSpec(memory_space=pl.ANY)] * (held is not None),
        out_specs=pl.BlockSpec((HALF, 2 * PW), lambda i: (part, 0)),
        input_output_aliases={} if held is None else {7: 0},
        compiler_params=pltpu.CompilerParams(vmem_limit_bytes=16 * 2**20),
        name="owned_rows",
    )(*args)


def on_slice(coupling, scen_kkt, active_rows, first_hess):
    panel_cols = 2 * PW
    scen_idx = lax.axis_index("scen")
    core, spot = scen_idx % 2, scen_idx // 2
    side = lax.axis_index("grp") % 2

    def where_of(core_bit):
        slabs = [scen_idx ^ (y * 4 + x * 2 + core_bit) for x in range(2) for y in range(2)]
        return jnp.stack(slabs + [side]).astype(jnp.int32)

    wheres = [where_of(0), where_of(1)]
    perm = jnp.stack([(spot ^ m) * 2 + (core ^ c) for c in range(2) for m in range(4)])
    perm = perm.astype(jnp.int32)
    scen_kkt = after(scen_kkt, *wheres, perm)
    xt = scen_solve(scen_kkt, coupling, active_rows, panel_cols)

    packed = pivot_prod(xt, coupling)
    away = panel_products(wheres[1], xt, coupling, packed)
    got = [flip(piece, "scen", 1) for piece in away]
    keeps = panel_products(wheres[0], after(xt, *away), coupling, packed)

    sends, token = [], []
    for i in range(3):
        sends.append(keeps[i][4:] + after(got[i], *token)[4:])
        token = [sends[i]]
    fresh = [flip(sends[i], *HOPS[ORDERS[i][0]]) for i in range(3)]
    keeps = [keeps[i][:4] + after(got[i], *sends)[:4] for i in range(3)]
    got = fresh
    got[0] = after(got[0], *keeps)
    sends, token = [], []
    for i in range(3):
        sends.append(keeps[i][2:] + after(got[i], *token)[2:])
        token = [sends[i]]
    fresh = [flip(sends[i], *HOPS[ORDERS[i][1]]) for i in range(3)]
    keeps = [keeps[i][:2] + after(got[i], *sends)[:2] for i in range(3)]
    got = fresh
    got[0] = after(got[0], *keeps)
    main = CUTS[1]
    unit = jnp.concatenate(
        [
            keeps[0][0, main:] + got[0][0, main:],
            keeps[0][1, main : main + UNIT - FIRST] + got[0][1, main : main + UNIT - FIRST],
        ],
        0,
    )
    keeps[0], got[0] = keeps[0][:, :main], got[0][:, :main]
    sends, token = [], []
    for i in range(3):
        sends.append(keeps[i][1:] + after(got[i], *token)[1:])
        token = [sends[0], unit]
    fresh = [flip(sends[i], *HOPS[ORDERS[i][2]]) for i in range(3)]
    over_z = flip(unit, "grp", 1)
    keeps = [keeps[i][:1] + after(got[i], *sends)[:1] for i in range(3)]
    unit = unit + after(over_z, *keeps)
    over_z = flip(unit, "grp", 2)
    fresh = [after(f, unit) for f in fresh]
    slab = jnp.concatenate([keeps[i][0] + fresh[i][0] for i in range(3)], 0)
    parts = [slab[:, part * HALF : (part + 1) * HALF] for part in range(2)]
    unit = unit + after(over_z, *parts)
    rest = [unit] + [flip(unit, "scen", 2 * mask) for mask in (1, 2, 3)]

    got_one = flip(parts[0], "grp", 2)
    pivot_half = jnp.concatenate(rest, 0)
    pivot_other = flip(pivot_half, "scen", 1)
    one = parts[0] + after(got_one, pivot_half)
    one_other = flip(one, "grp", 1)
    got_two = flip(after(parts[1], one), "grp", 2)
    wt1, l1, u, left = pivot_one(perm, first_hess, after(pivot_half, one), pivot_other)
    wt2, l2 = pivot_two(wt1, u, left)
    two = parts[1] + after(got_two, left)
    two_other = flip(two, "grp", 1)
    where = jnp.stack([side, scen_idx]).astype(jnp.int32)
    inverse = (wt1, wt2, l1, l2)
    rows = final_rows(where, inverse, one, after(one_other, two, wt2), 0)
    return final_rows(where, inverse, two, after(two_other, rows), 1, rows)


def any_mesh(coupling, scen_kkt, active_rows, first_hess):
    panel_cols = 2 * PW
    own_rows = coupling.shape[2] // lax.axis_size("scen")
    start = lax.axis_index("scen") * own_rows
    xt = scen_solve(scen_kkt, coupling, active_rows, panel_cols)
    packed = lax.psum(pivot_prod(xt, coupling), ("scen", "grp"))
    wt1, l1, u, left = pivot_one(jnp.zeros((1,), jnp.int32), first_hess, packed)
    wt2, l2 = pivot_two(wt1, u, left)
    own = lax.psum_scatter(
        dot(xt, coupling[0], None), "scen", scatter_dimension=1, tiled=True
    )
    own = lax.psum(own, "grp")
    rows = jnp.concatenate([dotT(own[:PW], wt1), dotT(own, wt2)], 1)
    factor = jnp.concatenate([l1, jnp.concatenate([jnp.zeros_like(l2), l2], 0)], 1)
    padded = jnp.concatenate([factor, jnp.zeros((own_rows, panel_cols), jnp.float32)], 0)
    head = lax.dynamic_slice_in_dim(padded, jnp.minimum(start, panel_cols), own_rows)
    global_row = start + lax.broadcasted_iota(jnp.int32, (own_rows, 1), 0)
    return jnp.where(global_row < panel_cols, head, rows)


def solution(mesh):
    placed = (
        P(("scen", "grp"), None, None),
        P(("scen", "grp"), None, None),
        P(("scen", "grp")),
        P(),
    )
    whole = mesh.shape["scen"] == 8 and mesh.shape["grp"] == 4
    return jax.shard_map(
        on_slice if whole else any_mesh,
        mesh=mesh,
        in_specs=placed,
        out_specs=P("scen", None),
        check_vma=False,
    )
```

```python
import functools

import jax
import jax.numpy as jnp
from jax import lax
from jax.experimental import pallas as pl
from jax.experimental.pallas import tpu as pltpu
from jax.sharding import PartitionSpec as P

PW = 256
HALF = 256
CUTS = (0, 72, 168, 256)
UNIT = 40
FIRST = 24
H=lax.Precision.HIGHEST
def bc(x,s): return jnp.broadcast_to(x[s:s+1,:], x.shape)
def halves(x):
    hi=x.astype(jnp.bfloat16)
    return hi,(x-hi.astype(jnp.float32)).astype(jnp.bfloat16)
def dot3(a,b,dims):
    (i,),(j,)=dims
    ah,al=halves(a); bh,bl=halves(b)
    return lax.dot_general(jnp.concatenate([ah,ah,al],i),jnp.concatenate([bh,bl,bh],j),(dims,((),())),preferred_element_type=jnp.float32)
def elim(R, off, nb):
    ng=nb//8; nh=len(R[0])
    row=lax.broadcasted_iota(jnp.int32,(8,128),0)
    L={}
    for j in range(nb):
        for g in range(j//8,ng):
            L[j,g]=jnp.broadcast_to(R[g][0][:,off+j:off+j+1],(8,128))
    out=[None]*ng
    a=bc(L[0,0],0); b=bc(L[0,0],1); c=bc(L[1,0],1)
    for j in range(0,nb,2):
        gj=j//8; s=j%8
        det=a*c-b*b
        rd=1.0/det
        al={}; be={}
        for g in range(gj,ng):
            x=L[j,g]*c-L[j+1,g]*b; y=L[j+1,g]*a-L[j,g]*b
            if g==gj:
                x=jnp.where(row>s+1,x,0.0); y=jnp.where(row>s+1,y,0.0)
            al[g]=x; be[g]=y
        nxt=None
        if j+2<nb:
            k=j+2; g=k//8; t=k%8
            p,q,p2,q2=bc(L[j,g],t),bc(L[j+1,g],t),bc(L[j,g],t+1),bc(L[j+1,g],t+1)
            x,y,x2,y2=bc(al[g],t),bc(be[g],t),bc(al[g],t+1),bc(be[g],t+1)
            nxt=(bc(L[k,g],t)-(x*p+y*q)*rd, bc(L[k,g],t+1)-(x2*p+y2*q)*rd, bc(L[k+1,g],t+1)-(x2*p2+y2*q2)*rd)
        for k in range(j+2,nb):
            p=bc(L[j,k//8],k%8); q=bc(L[j+1,k//8],k%8)
            for g in range(k//8,ng):
                L[k,g]=L[k,g]-(al[g]*p+be[g]*q)*rd
        r1=[bc(R[gj][h],s) for h in range(nh)]; r2=[bc(R[gj][h],s+1) for h in range(nh)]
        ra=1.0/a
        sa=lax.rsqrt(a); sb=lax.rsqrt(det*ra); ba=b*ra
        if s==0: out[gj]=[jnp.zeros((8,128),jnp.float32)]*nh
        for h in range(nh):
            out[gj][h]=jnp.where(row==s,r1[h]*sa,jnp.where(row==s+1,(r2[h]-ba*r1[h])*sb,out[gj][h]))
        for g in range(gj,ng):
            if g==gj and s==6: continue
            x=al[g]*rd; y=be[g]*rd
            R[g]=[R[g][h]-(x*r1[h]+y*r2[h]) for h in range(nh)]
        if nxt: a,b,c=nxt
    return out
def base128(A, exact=False, nb=32, between=None):
    row=lax.broadcasted_iota(jnp.int32,(8,128),0); lane=lax.broadcasted_iota(jnp.int32,(8,128),1)
    M=[[A[8*g:8*g+8,:],jnp.where(lane==row+8*g,1.0,0.0)] for g in range(16)]
    outs=[]
    n=128//nb; ng=nb//8
    for c in range(n):
        if between: between[c]()
        o=elim(M[c*ng:(c+1)*ng],c*nb,nb)
        outs+=o
        if c<n-1:
            O=[jnp.concatenate([o[g][h] for g in range(ng)],0) for h in range(2)]
            O2=jnp.concatenate(O,1)
            dims=((0,),(0,))
            if exact: T=lax.dot_general(O[0],O2,(dims,((),())),precision=H,preferred_element_type=jnp.float32)
            else: T=dot3(O[0],O2,dims)
            for g in range((c+1)*ng,16):
                M[g]=[M[g][h]-T[8*g:8*g+8,128*h:128*h+128] for h in range(2)]
    return [jnp.concatenate([outs[g][h] for g in range(16)],0) for h in range(2)]
BS=128
def dotT(a,b,prec=H): return lax.dot_general(a,b,(((0,),(0,)),((),())),precision=prec,preferred_element_type=jnp.float32)
def dot(a,b,prec=H): return lax.dot_general(a,b,(((1,),(0,)),((),())),precision=prec,preferred_element_type=jnp.float32)
def blk(k): return slice(k*BS,(k+1)*BS)
def sym(a): return 0.5*(a+a.T)
def upper_blocks(m): return [(i,j) for i in range(m) for j in range(i,m)]
def packed_places(m):
    places,slots={},[]
    blocks=upper_blocks(m)
    full=len(blocks)//m*m
    for q,ij in enumerate(blocks[:full]): places[ij]=[(0,q//m*BS,q%m,BS)]
    rest=blocks[full:]
    cut=BS*len(rest)//m
    for q,ij in enumerate(rest):
        per=BS//cut
        places[ij]=[(t*cut,full//m*BS,q*per+t,cut) for t in range(per)]
    return places,full//m*BS+(cut if rest else 0)
def lanes(g): return slice(g*BS,(g+1)*BS)
def fetch_slabs(ids_ref,core_bit,c_hbm,slabs,sems):
    own=slabs.shape[2]
    copies=[]
    for s in range(4):
        slab=ids_ref[0]^(s%2*4+s//2*2+core_bit)
        cols=pl.ds(pl.multiple_of(slab*own,own),own)
        copies.append(pltpu.make_async_copy(c_hbm.at[0,:,cols],slabs.at[s],sems.at[s]))
        copies[-1].start()
    return copies
def slab_products(ids_ref,core_bit,xt_ref,packed_ref,slabs,copies,stages,outs,sems):
    a,b,z=stages
    main,rest=CUTS[1],UNIT-FIRST
    pending=[]
    for s in range(4):
        slab=ids_ref[0]^(s%2*4+s//2*2+core_bit)
        copies[s].wait()
        total=dot(xt_ref[...],slabs[s],None)
        for half in range(2):
            to=pl.ds(ids_ref[1]^half,1)
            part=total[half*HALF:(half+1)*HALF,:]
            a[s,to,:main,:]=part[CUTS[0]:CUTS[1],:][None]
            b[s,to]=part[CUTS[1]:CUTS[2],:][None]
            z[s,to]=part[CUTS[2]:CUTS[3],:][None]
        unit=pl.multiple_of(slab*UNIT,8)
        a[s,0,main:,:]=packed_ref[pl.ds(unit,FIRST),:]
        a[s,1,main:main+rest,:]=packed_ref[pl.ds(unit+FIRST,rest),:]
        a[s,1,main+rest:,:]=jnp.zeros((FIRST-rest,a.shape[3]),jnp.float32)
        x,y=s//2,s%2
        to=(outs[0].at[x,y],outs[1].at[y,:,x],outs[2].at[:,x,y])
        for i in range(3):
            pending.append(pltpu.make_async_copy(stages[i].at[s],to[i],sems.at[s,i]))
            pending[-1].start()
    for copy in pending: copy.wait()
def slab_shapes(own):
    high=[CUTS[1]+FIRST,CUTS[2]-CUTS[1],CUTS[3]-CUTS[2]]
    outs=[jax.ShapeDtypeStruct((2,2,2,h,own),jnp.float32) for h in high]
    stages=[pltpu.VMEM((4,2,h,own),jnp.float32) for h in high]
    return outs,stages
def pack_pivot(x,panel,packed_ref):
    n=x.shape[0]; half=n//2; per=half//BS
    T=dot(x,panel,None)
    D=[sym(T[:half,:half]),sym(T[half:,half:])]
    for (i,j),where in packed_places(n//BS)[0].items():
        if i//per==j//per: v=D[i//per][blk(i%per),blk(j%per)]
        else: v=T[blk(i),blk(j)]
        for r,row,g,rows in where: packed_ref[row:row+rows,lanes(g)]=v[r:r+rows,:]
def scen_kernel(ids_ref,act_ref,k_ref,c_hbm,x_ref,packed_ref,*refs,away):
    outs,refs=refs[:3*away],refs[3*away:]
    M,D,Wk,left,right,row_ref,inv_ref,panel_ref,sem=refs[:9]
    n=k_ref.shape[1]; nblk=n//BS
    fetch=pltpu.make_async_copy(c_hbm.at[0,:,0:panel_ref.shape[1]],panel_ref,sem)
    fetch.start()
    if away:
        slabs,stages,in_sems,out_sems=refs[9],refs[10:13],refs[13],refs[14]
        copies=fetch_slabs(ids_ref,1,c_hbm,slabs,in_sems)
    M[...]=k_ref[0].astype(jnp.float32)
    D[...]=k_ref[0,0:BS,0:BS].astype(jnp.float32)
    Wk[...]=jnp.zeros_like(Wk)
    eye=jnp.where(lax.broadcasted_iota(jnp.int32,(BS,BS),0)==lax.broadcasted_iota(jnp.int32,(BS,BS),1),1.0,0.0)
    def sweep(k,live):
        here=pl.ds(pl.multiple_of(k*BS,BS),BS)
        def invert():
            W=Wk[...]
            inv_ref[...]=dotT(W,W)
            col_hi,col_lo=halves(jnp.where(live,M[:,here],0.0))
            left[:,0:BS]=col_hi; left[:,BS:2*BS]=col_hi; left[:,2*BS:]=col_lo
            left[here,:]=jnp.zeros((BS,3*BS),jnp.bfloat16)
        def scale():
            inv=inv_ref[...]
            row=dot3(inv,M[here,:],((1,),(0,)))
            row_ref[...]=row
            row_ref[:,here]=eye-inv
            hi,lo=halves(row_ref[...])
            right[0:BS,:]=hi; right[BS:2*BS,:]=lo; right[2*BS:,:]=hi
            row_ref[...]=row
            row_ref[:,here]=-inv
        def spread(rows):
            M[rows,:]=M[rows,:]-dot(left[rows,:],right[...],None)
        def first(): spread(slice(0,n//2))
        def second():
            spread(slice(n//2,n))
            M[here,:]=jnp.where(live,row_ref[...],M[here,:])
        return invert,scale,first,second
    def step(k,_):
        here=pl.ds(pl.multiple_of(k*BS,BS),BS)
        follow=pl.ds(pl.multiple_of(jnp.minimum(k+1,nblk-1)*BS,BS),BS)
        _,W=base128(D[...],between=sweep(jnp.maximum(k-1,0),k>0))
        P=dot3(W,M[here,follow],((1,),(0,)))
        D[...]=M[follow,follow]-dot3(P,P,((0,),(0,)))
        Wk[...]=W
        return 0
    lax.fori_loop(0,nblk,step,0)
    for part in sweep(nblk-1,True): part()
    fetch.wait()
    panel=panel_ref[...]
    kept=lax.broadcasted_iota(jnp.int32,(n,1),0)<act_ref[0]
    masked=jnp.where(kept,panel,jnp.zeros((),jnp.bfloat16))
    hi,lo=halves(M[...])
    x=dotT(masked,hi,None)+dotT(masked,lo,None)
    kept=lax.broadcasted_iota(jnp.int32,(1,n),1)<act_ref[0]
    x=jnp.where(kept,-x,0.0).astype(jnp.bfloat16)
    x_ref[...]=x
    pack_pivot(x,panel,packed_ref)
    if away: slab_products(ids_ref,1,x_ref,packed_ref,slabs,copies,stages,outs,out_sems)
def scen_solve(ids,kkt,coupling,active,cols,own=0):
    n=kkt.shape[1]
    vm=pltpu.VMEM; dma=pltpu.SemaphoreType.DMA
    smem,vmem,any_=(pl.BlockSpec(memory_space=m) for m in (pltpu.SMEM,vm,pl.ANY))
    out_shape=[jax.ShapeDtypeStruct((cols,n),jnp.bfloat16),jax.ShapeDtypeStruct((packed_places(cols//BS)[1],cols),jnp.float32)]
    scratch=[vm((n,n),jnp.float32),vm((BS,BS),jnp.float32),vm((BS,BS),jnp.float32),vm((n,3*BS),jnp.bfloat16),
        vm((3*BS,n),jnp.bfloat16),vm((BS,n),jnp.float32),vm((BS,BS),jnp.float32),vm((n,cols),jnp.bfloat16),dma]
    if own:
        outs,stages=slab_shapes(own)
        out_shape+=outs
        scratch+=[vm((4,n,own),jnp.bfloat16)]+stages+[dma((4,)),dma((4,3))]
    return pl.pallas_call(functools.partial(scen_kernel,away=bool(own)),
        out_shape=out_shape,in_specs=[smem,smem,vmem,any_],out_specs=[vmem,vmem]+[any_]*(len(out_shape)-2),
        scratch_shapes=scratch,
        compiler_params=pltpu.CompilerParams(vmem_limit_bytes=52*2**20),
        name="scen_solve")(ids,active,kkt,coupling)
def kept_kernel(ids_ref,xt_ref,packed_ref,c_hbm,*refs):
    outs,slabs,stages,in_sems,out_sems=refs[:3],refs[3],refs[4:7],refs[7],refs[8]
    copies=fetch_slabs(ids_ref,0,c_hbm,slabs,in_sems)
    slab_products(ids_ref,0,xt_ref,packed_ref,slabs,copies,stages,outs,out_sems)
def kept_products(ids,xt,packed,coupling,own):
    cols,n=xt.shape
    dma=pltpu.SemaphoreType.DMA
    smem,vmem,any_=(pl.BlockSpec(memory_space=m) for m in (pltpu.SMEM,pltpu.VMEM,pl.ANY))
    outs,stages=slab_shapes(own)
    return pl.pallas_call(kept_kernel,out_shape=outs,in_specs=[smem,vmem,vmem,any_],out_specs=[any_]*3,
        scratch_shapes=[pltpu.VMEM((4,n,own),jnp.bfloat16)]+stages+[dma((4,)),dma((4,3))],
        cost_estimate=pl.CostEstimate(flops=8*own*cols*n,bytes_accessed=8*own*(n+4*cols),transcendentals=0),
        compiler_params=pltpu.CompilerParams(vmem_limit_bytes=40*2**20),
        name="kept_products")(ids,xt,packed,coupling)
def panel_factor(A,wt_ref,l_ref,base):
    n=A.shape[1]; end=base+2*BS
    eye=lax.broadcasted_iota(jnp.int32,(BS,BS),0)<=lax.broadcasted_iota(jnp.int32,(BS,BS),1)
    WT=[]
    for k in range(2):
        lo=base+k*BS; me=slice(lo,lo+BS)
        Uk,Wk=base128(A[me,me])
        WT.append(Wk.T)
        l_ref[lo-base:lo-base+BS,blk(k)]=jnp.where(eye,Uk,0.0).T
        if lo+BS<n:
            P=dot3(Wk,A[me,lo+BS:],((1,),(0,)))
            A[me,lo+BS:]=P
            for i in range((n-lo)//BS-1):
                r=lo+(i+1)*BS
                if r<end: A[r:r+BS,r:]=A[r:r+BS,r:]-dot3(P[:,i*BS:(i+1)*BS],P[:,i*BS:],((0,),(0,)))
                l_ref[r-base:r-base+BS,blk(k)]=P[:,i*BS:(i+1)*BS].T
    l_ref[0:BS,blk(1)]=jnp.zeros((BS,BS),jnp.float32)
    top=wt_ref.shape[0]-2*BS
    wt_ref[top:top+BS,blk(0)]=WT[0]
    wt_ref[top+BS:,blk(0)]=jnp.zeros((BS,BS),jnp.float32)
    wt_ref[top:top+BS,blk(1)]=-dot3(dot3(WT[0],A[base:base+BS,base+BS:end],((1,),(0,))),WT[1],((1,),(0,)))
    wt_ref[top+BS:,blk(1)]=WT[1]
def pivot_one_kernel(ids_ref,hess_ref,*refs):
    srcs,(wt_ref,l_ref,u_ref,rest_ref,A,pk)=refs[:-6],refs[-6:]
    n=A.shape[0]; nblk=n//BS; half=n//2
    if len(srcs)==1: pk[...]=srcs[0][...]
    else:
        for m,src in enumerate(srcs):
            for c in range(2):
                unit=ids_ref[0]^(2*m+c)
                pk[pl.ds(pl.multiple_of(unit*UNIT,8),UNIT),:]=src[c*UNIT:(c+1)*UNIT,:]
    diag=lax.broadcasted_iota(jnp.int32,(BS,BS),0)==lax.broadcasted_iota(jnp.int32,(BS,BS),1)
    for (i,j),where in packed_places(nblk)[0].items():
        parts=[pk[row:row+high,lanes(g)] for _,row,g,high in where]
        v=parts[0] if len(parts)==1 else jnp.concatenate(parts,0)
        A[blk(i),blk(j)]=v+jnp.where(diag,hess_ref[:,blk(i)],0.0) if i==j else v
    panel_factor(A,wt_ref,l_ref,0)
    u=A[0:half,half:]
    u_ref[...]=u
    for k in range(half//BS):
        o=k*BS
        rest_ref[o:o+BS,o:]=A[half+o:half+o+BS,half+o:]-dot3(u[:,o:o+BS],u[:,o:],((0,),(0,)))
    rest_ref[BS:,0:BS]=jnp.zeros((BS,BS),jnp.float32)
def pivot_one(ids,hess,*srcs):
    n=hess.shape[0]; total=sum(s.shape[0] for s in srcs)
    sd=lambda r,c: jax.ShapeDtypeStruct((r,c),jnp.float32)
    vm=pl.BlockSpec(memory_space=pltpu.VMEM)
    return pl.pallas_call(pivot_one_kernel,out_shape=[sd(n//2,n//2),sd(n,n//2),sd(n//2,n//2),sd(n//2,n//2)],
        in_specs=[pl.BlockSpec(memory_space=pltpu.SMEM)]+[vm]*(1+len(srcs)),out_specs=[vm]*4,
        scratch_shapes=[pltpu.VMEM((n,n),jnp.float32),pltpu.VMEM((total,n),jnp.float32)],
        cost_estimate=pl.CostEstimate(flops=1,bytes_accessed=1,transcendentals=0),
        compiler_params=pltpu.CompilerParams(vmem_limit_bytes=16*2**20),name="pivot_one")(ids,hess[None],*srcs)
def own_rows(ids_ref,wt1_ref,wt2_ref,l1_ref,l2_ref,*refs):
    out_ref=refs[-1]
    @pl.when(ids_ref[0]==0)
    def _():
        out_ref[:,:PW]=l1_ref[...]
        out_ref[:PW,PW:]=jnp.zeros_like(l2_ref)
        out_ref[PW:,PW:]=l2_ref[...]
    @pl.when(ids_ref[0]>0)
    def _():
        rows=((0,),(0,))
        swap=ids_ref[1]>0
        per=len(refs)//2
        high=out_ref.shape[0]//per
        for part in range(per):
            mine,other=refs[2*part][...],refs[2*part+1][...]
            panel=jnp.concatenate([jnp.where(swap,other,mine),jnp.where(swap,mine,other)],0)
            to=slice(part*high,(part+1)*high)
            out_ref[to,:PW]=dot3(panel[:PW],wt1_ref[...],rows)
            out_ref[to,PW:]=dot3(panel,wt2_ref[...],rows)
def pivot_two_kernel(wt1_ref,u_ref,rest_ref,wt_ref,l_ref,A):
    half=wt1_ref.shape[0]
    A[...]=rest_ref[...]
    panel_factor(A,wt_ref,l_ref,0)
    wt_ref[0:half,:]=-dot3(wt1_ref[...],dot3(u_ref[...],wt_ref[half:,:],((1,),(0,))),((1,),(0,)))
def pivot_two(wt1,u,rest):
    half=wt1.shape[0]
    sd=lambda r,c: jax.ShapeDtypeStruct((r,c),jnp.float32)
    vm=pl.BlockSpec(memory_space=pltpu.VMEM)
    return pl.pallas_call(pivot_two_kernel,out_shape=[sd(2*half,half),sd(half,half)],
        in_specs=[vm]*3,out_specs=[vm]*2,scratch_shapes=[pltpu.VMEM((half,half),jnp.float32)],
        cost_estimate=pl.CostEstimate(flops=1,bytes_accessed=1,transcendentals=0),
        compiler_params=pltpu.CompilerParams(vmem_limit_bytes=16*2**20),name="pivot_two")(wt1,u,rest)


HOPS = {"x": ("scen", 2), "y": ("scen", 4), "z": ("grp", 1)}
ORDERS = ("xyz", "yzx", "zxy")


def flip(array, axis, mask):
    size = lax.axis_size(axis)
    return lax.ppermute(array, axis, [(i, i ^ mask) for i in range(size)])


def after(array, *others):
    return lax.optimization_barrier((array,) + others)[0]


def final_rows(ids, inverse, *halves):
    vmem = pl.BlockSpec(memory_space=pltpu.VMEM)
    return pl.pallas_call(
        own_rows,
        out_shape=jax.ShapeDtypeStruct((2 * HALF, 2 * PW), jnp.float32),
        in_specs=[pl.BlockSpec(memory_space=pltpu.SMEM)] + [vmem] * (4 + len(halves)),
        out_specs=vmem,
        compiler_params=pltpu.CompilerParams(vmem_limit_bytes=16 * 2**20),
        name="owned_rows",
    )(ids, *inverse, *halves)


def on_slice(coupling, scen_kkt, active_rows, first_hess):
    panel_cols = 2 * PW
    own = coupling.shape[2] // 8
    ids = jnp.stack([lax.axis_index("scen"), lax.axis_index("grp") % 2]).astype(jnp.int32)
    xt, packed, *away = scen_solve(ids, scen_kkt, coupling, active_rows, panel_cols, own)

    def blocks(pieces):
        return [piece.reshape((8,) + piece.shape[-2:]) for piece in pieces]

    got = [flip(piece, "scen", 1) for piece in blocks(away)]
    keeps = blocks(kept_products(ids, after(xt, *away), packed, coupling, own))

    sends, token = [], []
    for i in range(3):
        sends.append(keeps[i][4:] + after(got[i], *token)[4:])
        token = [sends[i]]
    fresh = [flip(sends[i], *HOPS[ORDERS[i][0]]) for i in range(3)]
    keeps = [keeps[i][:4] + after(got[i], *sends)[:4] for i in range(3)]
    got = fresh
    got[0] = after(got[0], *keeps)
    sends, token = [], []
    for i in range(3):
        sends.append(keeps[i][2:] + after(got[i], *token)[2:])
        token = [sends[i]]
    fresh = [flip(sends[i], *HOPS[ORDERS[i][1]]) for i in range(3)]
    keeps = [keeps[i][:2] + after(got[i], *sends)[:2] for i in range(3)]
    got = fresh
    got[0] = after(got[0], *keeps)
    main = CUTS[1]
    unit = jnp.concatenate(
        [
            keeps[0][0, main:] + got[0][0, main:],
            keeps[0][1, main : main + UNIT - FIRST] + got[0][1, main : main + UNIT - FIRST],
        ],
        0,
    )
    keeps[0], got[0] = keeps[0][:, :main], got[0][:, :main]
    sends, token = [jnp.concatenate([keeps[0][1] + got[0][1], unit], 0)], []
    for i in (1, 2):
        sends.append(keeps[i][1] + after(got[i], *sends)[1])
    fresh = [flip(sends[i], *HOPS[ORDERS[i][2]]) for i in range(3)]
    keeps = [keeps[i][0] + after(got[i], *sends)[0] for i in range(3)]
    unit = unit + after(fresh[0], *keeps)[main:]
    over_z = flip(unit, "grp", 2)
    unit = unit + after(over_z, unit)
    fresh = [after(f, unit) for f in fresh]
    slab = jnp.concatenate([keeps[0] + fresh[0][:main], keeps[1] + fresh[1], keeps[2] + fresh[2]], 0)
    got_far = flip(slab, "grp", 2)

    unit = after(unit, slab)
    pair = jnp.concatenate([unit, flip(unit, "scen", 1)], 0)
    pairs = [pair] + [flip(pair, "scen", 2 * m) for m in (1, 2, 3)]
    wt1, l1, u, left = pivot_one(ids, first_hess, *pairs)
    slab = slab + after(got_far, left)
    other = flip(slab, "grp", 1)
    wt2, l2 = pivot_two(wt1, u, after(left, slab))
    return final_rows(ids, (wt1, wt2, l1, l2), slab, after(other, wt2))


def any_mesh(coupling, scen_kkt, active_rows, first_hess):
    panel_cols = 2 * PW
    own_rows = coupling.shape[2] // lax.axis_size("scen")
    start = lax.axis_index("scen") * own_rows
    ids = jnp.zeros((2,), jnp.int32)
    xt, packed = scen_solve(ids, scen_kkt, coupling, active_rows, panel_cols)
    packed = lax.psum(packed, ("scen", "grp"))
    wt1, l1, u, left = pivot_one(ids, first_hess, packed)
    wt2, l2 = pivot_two(wt1, u, left)
    own = lax.psum_scatter(
        dot(xt, coupling[0], None), "scen", scatter_dimension=1, tiled=True
    )
    own = lax.psum(own, "grp")
    rows = jnp.concatenate([dotT(own[:PW], wt1), dotT(own, wt2)], 1)
    factor = jnp.concatenate([l1, jnp.concatenate([jnp.zeros_like(l2), l2], 0)], 1)
    padded = jnp.concatenate([factor, jnp.zeros((own_rows, panel_cols), jnp.float32)], 0)
    head = lax.dynamic_slice_in_dim(padded, jnp.minimum(start, panel_cols), own_rows)
    global_row = start + lax.broadcasted_iota(jnp.int32, (own_rows, 1), 0)
    return jnp.where(global_row < panel_cols, head, rows)


def solution(mesh):
    placed = (
        P(("scen", "grp"), None, None),
        P(("scen", "grp"), None, None),
        P(("scen", "grp")),
        P(),
    )
    whole = mesh.shape["scen"] == 8 and mesh.shape["grp"] == 4
    return jax.shard_map(
        on_slice if whole else any_mesh,
        mesh=mesh,
        in_specs=placed,
        out_specs=P("scen", None),
        check_vma=False,
    )
```

```python
import functools

import jax
import jax.numpy as jnp
from jax import lax
from jax.experimental import pallas as pl
from jax.experimental.pallas import tpu as pltpu
from jax.sharding import PartitionSpec as P

PW = 256
HALF = 256
CUTS = (0, 72, 168, 256)
UNIT = 40
FIRST = 24
H=lax.Precision.HIGHEST
def bc(x,s): return jnp.broadcast_to(x[s:s+1,:], x.shape)
def halves(x):
    hi=x.astype(jnp.bfloat16)
    return hi,(x-hi.astype(jnp.float32)).astype(jnp.bfloat16)
def dot3(a,b,dims):
    (i,),(j,)=dims
    ah,al=halves(a); bh,bl=halves(b)
    return lax.dot_general(jnp.concatenate([ah,ah,al],i),jnp.concatenate([bh,bl,bh],j),(dims,((),())),preferred_element_type=jnp.float32)
def elim(R, off, nb):
    ng=nb//8; nh=len(R[0])
    row=lax.broadcasted_iota(jnp.int32,(8,128),0)
    L={}
    for j in range(nb):
        for g in range(j//8,ng):
            L[j,g]=jnp.broadcast_to(R[g][0][:,off+j:off+j+1],(8,128))
    out=[None]*ng
    a=bc(L[0,0],0); b=bc(L[0,0],1); c=bc(L[1,0],1)
    for j in range(0,nb,2):
        gj=j//8; s=j%8
        det=a*c-b*b
        rd=1.0/det
        al={}; be={}
        for g in range(gj,ng):
            x=L[j,g]*c-L[j+1,g]*b; y=L[j+1,g]*a-L[j,g]*b
            if g==gj:
                x=jnp.where(row>s+1,x,0.0); y=jnp.where(row>s+1,y,0.0)
            al[g]=x; be[g]=y
        nxt=None
        if j+2<nb:
            k=j+2; g=k//8; t=k%8
            p,q,p2,q2=bc(L[j,g],t),bc(L[j+1,g],t),bc(L[j,g],t+1),bc(L[j+1,g],t+1)
            x,y,x2,y2=bc(al[g],t),bc(be[g],t),bc(al[g],t+1),bc(be[g],t+1)
            nxt=(bc(L[k,g],t)-(x*p+y*q)*rd, bc(L[k,g],t+1)-(x2*p+y2*q)*rd, bc(L[k+1,g],t+1)-(x2*p2+y2*q2)*rd)
        for k in range(j+2,nb):
            p=bc(L[j,k//8],k%8); q=bc(L[j+1,k//8],k%8)
            for g in range(k//8,ng):
                L[k,g]=L[k,g]-(al[g]*p+be[g]*q)*rd
        r1=[bc(R[gj][h],s) for h in range(nh)]; r2=[bc(R[gj][h],s+1) for h in range(nh)]
        ra=1.0/a
        sa=lax.rsqrt(a); sb=lax.rsqrt(det*ra); ba=b*ra
        if s==0: out[gj]=[jnp.zeros((8,128),jnp.float32)]*nh
        for h in range(nh):
            out[gj][h]=jnp.where(row==s,r1[h]*sa,jnp.where(row==s+1,(r2[h]-ba*r1[h])*sb,out[gj][h]))
        for g in range(gj,ng):
            if g==gj and s==6: continue
            x=al[g]*rd; y=be[g]*rd
            R[g]=[R[g][h]-(x*r1[h]+y*r2[h]) for h in range(nh)]
        if nxt: a,b,c=nxt
    return out
def base128(A, exact=False, nb=32, between=None):
    row=lax.broadcasted_iota(jnp.int32,(8,128),0); lane=lax.broadcasted_iota(jnp.int32,(8,128),1)
    M=[[A[8*g:8*g+8,:],jnp.where(lane==row+8*g,1.0,0.0)] for g in range(16)]
    outs=[]
    n=128//nb; ng=nb//8
    for c in range(n):
        if between: between[c]()
        o=elim(M[c*ng:(c+1)*ng],c*nb,nb)
        outs+=o
        if c<n-1:
            O=[jnp.concatenate([o[g][h] for g in range(ng)],0) for h in range(2)]
            O2=jnp.concatenate(O,1)
            dims=((0,),(0,))
            if exact: T=lax.dot_general(O[0],O2,(dims,((),())),precision=H,preferred_element_type=jnp.float32)
            else: T=dot3(O[0],O2,dims)
            for g in range((c+1)*ng,16):
                M[g]=[M[g][h]-T[8*g:8*g+8,128*h:128*h+128] for h in range(2)]
    return [jnp.concatenate([outs[g][h] for g in range(16)],0) for h in range(2)]
BS=128
def dotT(a,b,prec=H): return lax.dot_general(a,b,(((0,),(0,)),((),())),precision=prec,preferred_element_type=jnp.float32)
def dot(a,b,prec=H): return lax.dot_general(a,b,(((1,),(0,)),((),())),precision=prec,preferred_element_type=jnp.float32)
def blk(k): return slice(k*BS,(k+1)*BS)
def sym(a): return 0.5*(a+a.T)
def upper_blocks(m): return [(i,j) for i in range(m) for j in range(i,m)]
def packed_places(m):
    places,slots={},[]
    blocks=upper_blocks(m)
    full=len(blocks)//m*m
    for q,ij in enumerate(blocks[:full]): places[ij]=[(0,q//m*BS,q%m,BS)]
    rest=blocks[full:]
    cut=BS*len(rest)//m
    for q,ij in enumerate(rest):
        per=BS//cut
        places[ij]=[(t*cut,full//m*BS,q*per+t,cut) for t in range(per)]
    return places,full//m*BS+(cut if rest else 0)
def lanes(g): return slice(g*BS,(g+1)*BS)
def fetch_slabs(ids_ref,core_bit,c_hbm,slabs,sems):
    own=slabs.shape[2]
    copies=[]
    for s in range(4):
        slab=ids_ref[0]^(s%2*4+s//2*2+core_bit)
        cols=pl.ds(pl.multiple_of(slab*own,own),own)
        copies.append(pltpu.make_async_copy(c_hbm.at[0,:,cols],slabs.at[s],sems.at[s]))
        copies[-1].start()
    return copies
def slab_products(ids_ref,core_bit,xt_ref,packed_ref,slabs,copies,stages,outs,sems):
    a,b,z=stages
    main,rest=CUTS[1],UNIT-FIRST
    pending=[]
    for s in range(4):
        slab=ids_ref[0]^(s%2*4+s//2*2+core_bit)
        copies[s].wait()
        total=dot(xt_ref[...],slabs[s],None)
        for half in range(2):
            to=pl.ds(ids_ref[1]^half,1)
            part=total[half*HALF:(half+1)*HALF,:]
            a[s,to,:main,:]=part[CUTS[0]:CUTS[1],:][None]
            b[s,to]=part[CUTS[1]:CUTS[2],:][None]
            z[s,to]=part[CUTS[2]:CUTS[3],:][None]
        unit=pl.multiple_of(slab*UNIT,8)
        a[s,0,main:,:]=packed_ref[pl.ds(unit,FIRST),:]
        a[s,1,main:main+rest,:]=packed_ref[pl.ds(unit+FIRST,rest),:]
        a[s,1,main+rest:,:]=jnp.zeros((FIRST-rest,a.shape[3]),jnp.float32)
        x,y=s//2,s%2
        to=(outs[0].at[x,y],outs[1].at[y,:,x],outs[2].at[:,x,y])
        for i in range(3):
            pending.append(pltpu.make_async_copy(stages[i].at[s],to[i],sems.at[s,i]))
            pending[-1].start()
    for copy in pending: copy.wait()
def slab_shapes(own):
    high=[CUTS[1]+FIRST,CUTS[2]-CUTS[1],CUTS[3]-CUTS[2]]
    outs=[jax.ShapeDtypeStruct((2,2,2,h,own),jnp.float32) for h in high]
    stages=[pltpu.VMEM((4,2,h,own),jnp.float32) for h in high]
    return outs,stages
def pack_pivot(x,panel,packed_ref):
    n=x.shape[0]; half=n//2; per=half//BS
    T=dot(x,panel,None)
    D=[sym(T[:half,:half]),sym(T[half:,half:])]
    for (i,j),where in packed_places(n//BS)[0].items():
        if i//per==j//per: v=D[i//per][blk(i%per),blk(j%per)]
        else: v=T[blk(i),blk(j)]
        for r,row,g,rows in where: packed_ref[row:row+rows,lanes(g)]=v[r:r+rows,:]
def scen_kernel(ids_ref,act_ref,k_ref,c_hbm,x_ref,packed_ref,*refs,away):
    outs,refs=refs[:3*away],refs[3*away:]
    M,D,Wk,left,right,row_ref,inv_ref,panel_ref,sem=refs[:9]
    n=k_ref.shape[1]; nblk=n//BS
    fetch=pltpu.make_async_copy(c_hbm.at[0,:,0:panel_ref.shape[1]],panel_ref,sem)
    fetch.start()
    if away:
        slabs,stages,in_sems,out_sems=refs[9],refs[10:13],refs[13],refs[14]
        copies=fetch_slabs(ids_ref,1,c_hbm,slabs,in_sems)
    M[...]=k_ref[0].astype(jnp.float32)
    D[...]=k_ref[0,0:BS,0:BS].astype(jnp.float32)
    Wk[...]=jnp.zeros_like(Wk)
    eye=jnp.where(lax.broadcasted_iota(jnp.int32,(BS,BS),0)==lax.broadcasted_iota(jnp.int32,(BS,BS),1),1.0,0.0)
    def sweep(k,live):
        here=pl.ds(pl.multiple_of(k*BS,BS),BS)
        def invert():
            W=Wk[...]
            inv_ref[...]=dotT(W,W)
            col_hi,col_lo=halves(jnp.where(live,M[:,here],0.0))
            left[:,0:BS]=col_hi; left[:,BS:2*BS]=col_hi; left[:,2*BS:]=col_lo
            left[here,:]=jnp.zeros((BS,3*BS),jnp.bfloat16)
        def scale():
            inv=inv_ref[...]
            row=dot3(inv,M[here,:],((1,),(0,)))
            row_ref[...]=row
            row_ref[:,here]=eye-inv
            hi,lo=halves(row_ref[...])
            right[0:BS,:]=hi; right[BS:2*BS,:]=lo; right[2*BS:,:]=hi
            row_ref[...]=row
            row_ref[:,here]=-inv
        def spread(rows):
            M[rows,:]=M[rows,:]-dot(left[rows,:],right[...],None)
        def first(): spread(slice(0,n//2))
        def second():
            spread(slice(n//2,n))
            M[here,:]=jnp.where(live,row_ref[...],M[here,:])
        return invert,scale,first,second
    def step(k,_):
        here=pl.ds(pl.multiple_of(k*BS,BS),BS)
        follow=pl.ds(pl.multiple_of(jnp.minimum(k+1,nblk-1)*BS,BS),BS)
        _,W=base128(D[...],between=sweep(jnp.maximum(k-1,0),k>0))
        P=dot3(W,M[here,follow],((1,),(0,)))
        D[...]=M[follow,follow]-dot3(P,P,((0,),(0,)))
        Wk[...]=W
        return 0
    lax.fori_loop(0,nblk,step,0)
    invert,scale=sweep(nblk-1,True)[:2]
    invert()
    last=blk(nblk-1)
    left[last,0:BS]=(-eye).astype(jnp.bfloat16)
    fetch.wait()
    panel=panel_ref[...]
    kept=lax.broadcasted_iota(jnp.int32,(n,1),0)<act_ref[0]
    masked=jnp.where(kept,panel,jnp.zeros((),jnp.bfloat16))
    hi,lo=halves(M[0:n-BS,:])
    x=dotT(masked[0:n-BS],hi,None)+dotT(masked[0:n-BS],lo,None)
    scale()
    spread=dotT(masked,left[:,0:BS],None)+dotT(masked,left[:,2*BS:],None)
    hi,lo=halves(spread)
    x=x-dot(jnp.concatenate([hi,hi,lo],1),right[...],None)
    x=x-jnp.concatenate([jnp.zeros((x.shape[0],n-BS),jnp.float32),masked[last].astype(jnp.float32).T],1)
    kept=lax.broadcasted_iota(jnp.int32,(1,n),1)<act_ref[0]
    x=jnp.where(kept,-x,0.0).astype(jnp.bfloat16)
    x_ref[...]=x
    pack_pivot(x,panel,packed_ref)
    if away: slab_products(ids_ref,1,x_ref,packed_ref,slabs,copies,stages,outs,out_sems)
def scen_solve(ids,kkt,coupling,active,cols,own=0):
    n=kkt.shape[1]
    vm=pltpu.VMEM; dma=pltpu.SemaphoreType.DMA
    smem,vmem,any_=(pl.BlockSpec(memory_space=m) for m in (pltpu.SMEM,vm,pl.ANY))
    out_shape=[jax.ShapeDtypeStruct((cols,n),jnp.bfloat16),jax.ShapeDtypeStruct((packed_places(cols//BS)[1],cols),jnp.float32)]
    scratch=[vm((n,n),jnp.float32),vm((BS,BS),jnp.float32),vm((BS,BS),jnp.float32),vm((n,3*BS),jnp.bfloat16),
        vm((3*BS,n),jnp.bfloat16),vm((BS,n),jnp.float32),vm((BS,BS),jnp.float32),vm((n,cols),jnp.bfloat16),dma]
    if own:
        outs,stages=slab_shapes(own)
        out_shape+=outs
        scratch+=[vm((4,n,own),jnp.bfloat16)]+stages+[dma((4,)),dma((4,3))]
    return pl.pallas_call(functools.partial(scen_kernel,away=bool(own)),
        out_shape=out_shape,in_specs=[smem,smem,vmem,any_],out_specs=[vmem,vmem]+[any_]*(len(out_shape)-2),
        scratch_shapes=scratch,
        compiler_params=pltpu.CompilerParams(vmem_limit_bytes=52*2**20),
        name="scen_solve")(ids,active,kkt,coupling)
def kept_kernel(ids_ref,xt_ref,packed_ref,c_hbm,*refs):
    outs,slabs,stages,in_sems,out_sems=refs[:3],refs[3],refs[4:7],refs[7],refs[8]
    copies=fetch_slabs(ids_ref,0,c_hbm,slabs,in_sems)
    slab_products(ids_ref,0,xt_ref,packed_ref,slabs,copies,stages,outs,out_sems)
def kept_products(ids,xt,packed,coupling,own):
    cols,n=xt.shape
    dma=pltpu.SemaphoreType.DMA
    smem,vmem,any_=(pl.BlockSpec(memory_space=m) for m in (pltpu.SMEM,pltpu.VMEM,pl.ANY))
    outs,stages=slab_shapes(own)
    return pl.pallas_call(kept_kernel,out_shape=outs,in_specs=[smem,vmem,vmem,any_],out_specs=[any_]*3,
        scratch_shapes=[pltpu.VMEM((4,n,own),jnp.bfloat16)]+stages+[dma((4,)),dma((4,3))],
        cost_estimate=pl.CostEstimate(flops=8*own*cols*n,bytes_accessed=8*own*(n+4*cols),transcendentals=0),
        compiler_params=pltpu.CompilerParams(vmem_limit_bytes=40*2**20),
        name="kept_products")(ids,xt,packed,coupling)
def panel_factor(A,wt_ref,l_ref,base):
    n=A.shape[1]; end=base+2*BS
    eye=lax.broadcasted_iota(jnp.int32,(BS,BS),0)<=lax.broadcasted_iota(jnp.int32,(BS,BS),1)
    WT=[]
    for k in range(2):
        lo=base+k*BS; me=slice(lo,lo+BS)
        Uk,Wk=base128(A[me,me])
        WT.append(Wk.T)
        l_ref[lo-base:lo-base+BS,blk(k)]=jnp.where(eye,Uk,0.0).T
        if lo+BS<n:
            P=dot3(Wk,A[me,lo+BS:],((1,),(0,)))
            A[me,lo+BS:]=P
            for i in range((n-lo)//BS-1):
                r=lo+(i+1)*BS
                if r<end: A[r:r+BS,r:]=A[r:r+BS,r:]-dot3(P[:,i*BS:(i+1)*BS],P[:,i*BS:],((0,),(0,)))
                l_ref[r-base:r-base+BS,blk(k)]=P[:,i*BS:(i+1)*BS].T
    l_ref[0:BS,blk(1)]=jnp.zeros((BS,BS),jnp.float32)
    top=wt_ref.shape[0]-2*BS
    wt_ref[top:top+BS,blk(0)]=WT[0]
    wt_ref[top+BS:,blk(0)]=jnp.zeros((BS,BS),jnp.float32)
    wt_ref[top:top+BS,blk(1)]=-dot3(dot3(WT[0],A[base:base+BS,base+BS:end],((1,),(0,))),WT[1],((1,),(0,)))
    wt_ref[top+BS:,blk(1)]=WT[1]
def pivot_one_kernel(ids_ref,hess_ref,*refs):
    srcs,(wt_ref,l_ref,u_ref,rest_ref,A,pk)=refs[:-6],refs[-6:]
    n=A.shape[0]; nblk=n//BS; half=n//2
    if len(srcs)==1: pk[...]=srcs[0][...]
    else:
        for m,src in enumerate(srcs):
            for c in range(2):
                unit=ids_ref[0]^(2*m+c)
                pk[pl.ds(pl.multiple_of(unit*UNIT,8),UNIT),:]=src[c*UNIT:(c+1)*UNIT,:]
    diag=lax.broadcasted_iota(jnp.int32,(BS,BS),0)==lax.broadcasted_iota(jnp.int32,(BS,BS),1)
    for (i,j),where in packed_places(nblk)[0].items():
        parts=[pk[row:row+high,lanes(g)] for _,row,g,high in where]
        v=parts[0] if len(parts)==1 else jnp.concatenate(parts,0)
        A[blk(i),blk(j)]=v+jnp.where(diag,hess_ref[:,blk(i)],0.0) if i==j else v
    panel_factor(A,wt_ref,l_ref,0)
    u=A[0:half,half:]
    u_ref[...]=u
    for k in range(half//BS):
        o=k*BS
        rest_ref[o:o+BS,o:]=A[half+o:half+o+BS,half+o:]-dot3(u[:,o:o+BS],u[:,o:],((0,),(0,)))
    rest_ref[BS:,0:BS]=jnp.zeros((BS,BS),jnp.float32)
def pivot_one(ids,hess,*srcs):
    n=hess.shape[0]; total=sum(s.shape[0] for s in srcs)
    sd=lambda r,c: jax.ShapeDtypeStruct((r,c),jnp.float32)
    vm=pl.BlockSpec(memory_space=pltpu.VMEM)
    return pl.pallas_call(pivot_one_kernel,out_shape=[sd(n//2,n//2),sd(n,n//2),sd(n//2,n//2),sd(n//2,n//2)],
        in_specs=[pl.BlockSpec(memory_space=pltpu.SMEM)]+[vm]*(1+len(srcs)),out_specs=[vm]*4,
        scratch_shapes=[pltpu.VMEM((n,n),jnp.float32),pltpu.VMEM((total,n),jnp.float32)],
        cost_estimate=pl.CostEstimate(flops=1,bytes_accessed=1,transcendentals=0),
        compiler_params=pltpu.CompilerParams(vmem_limit_bytes=16*2**20),name="pivot_one")(ids,hess[None],*srcs)
def half_rows(wt1_ref,wt2_ref,panel,out_ref,first,held):
    rows=((0,),(0,))
    @pl.when(first)
    def _():
        left,right=dot3(panel,wt1_ref[...],rows),dot3(panel,wt2_ref[:PW],rows)
        out_ref[:,:PW]=left if held is None else held[:,:PW]+left
        out_ref[:,PW:]=right if held is None else held[:,PW:]+right
    @pl.when(jnp.logical_not(first))
    def _():
        right=dot3(panel,wt2_ref[PW:],rows)
        out_ref[:,:PW]=jnp.zeros_like(right) if held is None else held[:,:PW]
        out_ref[:,PW:]=right if held is None else held[:,PW:]+right
def mine_rows(ids_ref,wt1_ref,wt2_ref,mine_ref,out_ref):
    half_rows(wt1_ref,wt2_ref,mine_ref[...],out_ref,ids_ref[1]==0,None)
def own_rows(ids_ref,wt1_ref,wt2_ref,l1_ref,l2_ref,held_ref,other_ref,out_ref):
    @pl.when(ids_ref[0]==0)
    def _():
        out_ref[:,:PW]=l1_ref[...]
        out_ref[:PW,PW:]=jnp.zeros_like(l2_ref)
        out_ref[PW:,PW:]=l2_ref[...]
    @pl.when(ids_ref[0]>0)
    def _(): half_rows(wt1_ref,wt2_ref,other_ref[...],out_ref,ids_ref[1]>0,held_ref)
def pivot_two_kernel(wt1_ref,u_ref,rest_ref,wt_ref,l_ref,A):
    half=wt1_ref.shape[0]
    A[...]=rest_ref[...]
    panel_factor(A,wt_ref,l_ref,0)
    wt_ref[0:half,:]=-dot3(wt1_ref[...],dot3(u_ref[...],wt_ref[half:,:],((1,),(0,))),((1,),(0,)))
def pivot_two(wt1,u,rest):
    half=wt1.shape[0]
    sd=lambda r,c: jax.ShapeDtypeStruct((r,c),jnp.float32)
    vm=pl.BlockSpec(memory_space=pltpu.VMEM)
    return pl.pallas_call(pivot_two_kernel,out_shape=[sd(2*half,half),sd(half,half)],
        in_specs=[vm]*3,out_specs=[vm]*2,scratch_shapes=[pltpu.VMEM((half,half),jnp.float32)],
        cost_estimate=pl.CostEstimate(flops=1,bytes_accessed=1,transcendentals=0),
        compiler_params=pltpu.CompilerParams(vmem_limit_bytes=16*2**20),name="pivot_two")(wt1,u,rest)


HOPS = {"x": ("scen", 2), "y": ("scen", 4), "z": ("grp", 1)}
ORDERS = ("xyz", "yzx", "zxy")


def flip(array, axis, mask):
    size = lax.axis_size(axis)
    return lax.ppermute(array, axis, [(i, i ^ mask) for i in range(size)])


def after(array, *others):
    return lax.optimization_barrier((array,) + others)[0]


def final_rows(kernel, ids, *args):
    vmem = pl.BlockSpec(memory_space=pltpu.VMEM)
    return pl.pallas_call(
        kernel,
        out_shape=jax.ShapeDtypeStruct((2 * HALF, 2 * PW), jnp.float32),
        in_specs=[pl.BlockSpec(memory_space=pltpu.SMEM)] + [vmem] * len(args),
        out_specs=vmem,
        cost_estimate=pl.CostEstimate(flops=1, bytes_accessed=1, transcendentals=0),
        compiler_params=pltpu.CompilerParams(vmem_limit_bytes=16 * 2**20),
        name="owned_rows",
    )(ids, *args)


def on_slice(coupling, scen_kkt, active_rows, first_hess):
    panel_cols = 2 * PW
    own = coupling.shape[2] // 8
    ids = jnp.stack([lax.axis_index("scen"), lax.axis_index("grp") % 2]).astype(jnp.int32)
    xt, packed, *away = scen_solve(ids, scen_kkt, coupling, active_rows, panel_cols, own)

    def blocks(pieces):
        return [piece.reshape((8,) + piece.shape[-2:]) for piece in pieces]

    got = [flip(piece, "scen", 1) for piece in blocks(away)]
    keeps = blocks(kept_products(ids, after(xt, *away), packed, coupling, own))

    sends, token = [], []
    for i in range(3):
        sends.append(keeps[i][4:] + after(got[i], *token)[4:])
        token = [sends[i]]
    fresh = [flip(sends[i], *HOPS[ORDERS[i][0]]) for i in range(3)]
    keeps = [keeps[i][:4] + after(got[i], *sends)[:4] for i in range(3)]
    got = fresh
    got[0] = after(got[0], *keeps)
    sends, token = [], []
    for i in range(3):
        sends.append(keeps[i][2:] + after(got[i], *token)[2:])
        token = [sends[i]]
    fresh = [flip(sends[i], *HOPS[ORDERS[i][1]]) for i in range(3)]
    keeps = [keeps[i][:2] + after(got[i], *sends)[:2] for i in range(3)]
    got = fresh
    got[0] = after(got[0], *keeps)
    main = CUTS[1]
    unit = jnp.concatenate(
        [
            keeps[0][0, main:] + got[0][0, main:],
            keeps[0][1, main : main + UNIT - FIRST] + got[0][1, main : main + UNIT - FIRST],
        ],
        0,
    )
    keeps[0], got[0] = keeps[0][:, :main], got[0][:, :main]
    sends, token = [jnp.concatenate([keeps[0][1] + got[0][1], unit], 0)], []
    for i in (1, 2):
        sends.append(keeps[i][1] + after(got[i], *sends)[1])
    fresh = [flip(sends[i], *HOPS[ORDERS[i][2]]) for i in range(3)]
    keeps = [keeps[i][0] + after(got[i], *sends)[0] for i in range(3)]
    unit = unit + after(fresh[0], *keeps)[main:]
    over_z = flip(unit, "grp", 2)
    unit = unit + after(over_z, unit)
    fresh = [after(f, unit) for f in fresh]
    slab = jnp.concatenate([keeps[0] + fresh[0][:main], keeps[1] + fresh[1], keeps[2] + fresh[2]], 0)
    got_far = flip(slab, "grp", 2)

    unit = after(unit, slab)
    pair = jnp.concatenate([unit, flip(unit, "scen", 1)], 0)
    pairs = [pair] + [flip(pair, "scen", 2 * m) for m in (1, 2, 3)]
    wt1, l1, u, left = pivot_one(ids, first_hess, *pairs)
    slab = slab + after(got_far, left)
    other = flip(slab, "grp", 1)
    wt2, l2 = pivot_two(wt1, u, after(left, slab))
    held = final_rows(mine_rows, ids, wt1, wt2, slab)
    return final_rows(own_rows, ids, wt1, wt2, l1, l2, held, after(other, held))


def any_mesh(coupling, scen_kkt, active_rows, first_hess):
    panel_cols = 2 * PW
    own_rows = coupling.shape[2] // lax.axis_size("scen")
    start = lax.axis_index("scen") * own_rows
    ids = jnp.zeros((2,), jnp.int32)
    xt, packed = scen_solve(ids, scen_kkt, coupling, active_rows, panel_cols)
    packed = lax.psum(packed, ("scen", "grp"))
    wt1, l1, u, left = pivot_one(ids, first_hess, packed)
    wt2, l2 = pivot_two(wt1, u, left)
    own = lax.psum_scatter(
        dot(xt, coupling[0], None), "scen", scatter_dimension=1, tiled=True
    )
    own = lax.psum(own, "grp")
    rows = jnp.concatenate([dotT(own[:PW], wt1), dotT(own, wt2)], 1)
    factor = jnp.concatenate([l1, jnp.concatenate([jnp.zeros_like(l2), l2], 0)], 1)
    padded = jnp.concatenate([factor, jnp.zeros((own_rows, panel_cols), jnp.float32)], 0)
    head = lax.dynamic_slice_in_dim(padded, jnp.minimum(start, panel_cols), own_rows)
    global_row = start + lax.broadcasted_iota(jnp.int32, (own_rows, 1), 0)
    return jnp.where(global_row < panel_cols, head, rows)


def solution(mesh):
    placed = (
        P(("scen", "grp"), None, None),
        P(("scen", "grp"), None, None),
        P(("scen", "grp")),
        P(),
    )
    whole = mesh.shape["scen"] == 8 and mesh.shape["grp"] == 4
    return jax.shard_map(
        on_slice if whole else any_mesh,
        mesh=mesh,
        in_specs=placed,
        out_specs=P("scen", None),
        check_vma=False,
    )
```
